32 devices in a mesh: groups: 2 (over y), pair: 4 (over z), ri: 2 (over x), rep: 2 (over core).
Axes of the slice: x: 2, y: 2, z: 4, core: 2. Of those that a mesh axis runs over, the one named last changes fastest.
Arguments:
- b_int: bfloat16 [16, 12, 128, 640], P(('groups', 'ri'), None, 'pair'), parts along dimension 0, may hold values from -0.1875 to 0.1875
- gv_band: bfloat16 [24, 128, 1664], P(('groups', 'pair')), parts along dimension 0, may hold values from -0.25 to 0.25
- go_band: bfloat16 [24, 128, 640], P(('groups', 'pair'), 'rep'), parts along dimension 0, may hold values from -0.25 to 0.25
- mask: int32 [24, 5], P('groups'), parts along dimension 0, may hold values from 0 to 1, as said below
Outputs:
- chi: float32 [16, 8], P(('groups', 'ri')), parts along dimension 0
The draws below stay inside these ranges and needn't reach their ends.
There are 2 independent parts, one for each index of `groups`. The reference program is written for one: setup_inputs(seed, part) draws one part's arguments, and reference() takes and returns one part's arrays. A program takes and returns all parts, laid end to end along the dimension named above; each array names one. Nothing has to cross between parts.
Inputs may be any that keep to these rules, and one draw needn't show every extreme that they name: mask[I, 2] is 1 for every block I.
All inputs are finite; a program needn't handle non-finite values.
Results may differ from the reference program's by a relative error of at most 0.0045.
Values may be sent and summed in bfloat16 or wider, within the bound.
A program may use at most 64 MiB of HBM per device.

```python
import jax
import jax.numpy as jnp
from jax import lax

BS = 128
R = 2
NBLK = 12
RI = 8
NNB = 5
SPAN = 9
VBAND = 13


def draw_mask(key, part):
    key = jax.random.fold_in(key, 11)
    first_key, second_key = jax.random.split(key)
    density = jax.random.randint(first_key, (NBLK, 1), 1, 6)
    throws = jax.random.randint(second_key, (NBLK, 2 * R + 1), 0, 5)
    present = (throws < density).astype(jnp.int32)
    centre = (jnp.arange(2 * R + 1) == R)[None, :]
    return jnp.where(centre, 1, present).astype(jnp.int32)


def block_levels(key, shape, shards, low, top_value):
    gain, own = 1.0, jax.random.fold_in(key, 6)
    for dim, parts in shards:
        steps = jnp.exp(jax.random.uniform(jax.random.fold_in(own, dim), (parts,), jnp.float32, low / len(shards), top_value / len(shards)))
        gain = gain * jnp.repeat(steps, shape[dim] // parts).reshape([-1 if axis == dim else 1 for axis in range(len(shape))])
    return gain


def gaussian(stream_key, dims, width, reach, shards=(), kind=jnp.bfloat16):
    gain = block_levels(stream_key, dims, shards, -0.22, 0.18) if shards else 1.0
    array = jax.random.normal(stream_key, dims, jnp.float32) * width * gain
    return jnp.minimum(jnp.maximum(array, -reach), reach).astype(kind)


def setup_inputs(seed: int = 0, part: int = 0) -> dict:
    streams_of = jax.random.split(jax.random.key(seed), 5)
    part_keys = jax.random.split(jax.random.fold_in(streams_of[4], part), 5)
    b_int = gaussian(part_keys[0], (RI, NBLK, BS, NNB * BS), (BS * SPAN) ** -0.5, 0.1875, ((0, 2), (2, 4)))
    gv_band = gaussian(part_keys[1], (NBLK, BS, VBAND * BS), (BS * NNB) ** -0.5, 0.25, ((0, 4),))
    go_band = gaussian(part_keys[2], (NBLK, BS, NNB * BS), (BS * NNB) ** -0.5, 0.25, ((0, 4), (1, 2)))
    mask = draw_mask(jax.random.fold_in(jax.random.fold_in(streams_of[4], part), 71), part)
    return dict(b_int=b_int, gv_band=gv_band, go_band=go_band, mask=mask)


def reference(b_int, gv_band, go_band, mask):
    ri_count = b_int.shape[0]
    nblocks = b_int.shape[1]
    neighbours = 2 * R + 1
    window = 4 * R + 1
    shaped = b_int.reshape(ri_count, nblocks, BS, neighbours, BS)
    masked = (shaped * mask.astype(jnp.bfloat16)[None, :, None, :, None]).reshape(ri_count, nblocks, BS, neighbours * BS)

    def one_block(chi_sum, block_index):
        x_acc = jnp.zeros((ri_count, BS, window * BS), jnp.float32)
        y_acc = jnp.zeros((ri_count, BS, window * BS), jnp.float32)
        own_rows = lax.dynamic_index_in_dim(masked, block_index, 1, keepdims=False).astype(jnp.float32)
        occupied = lax.dynamic_index_in_dim(go_band, block_index, 0, keepdims=False).astype(jnp.float32)
        for offset in range(neighbours):
            neighbour_index = ((block_index + offset - R) % nblocks).astype(jnp.int32)
            virtual_rows = lax.dynamic_index_in_dim(gv_band, neighbour_index, 0, keepdims=False).astype(jnp.float32)
            x_acc = x_acc + jnp.einsum('pmn,nc->pmc', own_rows[:, :, offset * BS:(offset + 1) * BS],
                                       virtual_rows[:, (2 * R - offset) * BS:(6 * R - offset + 1) * BS])
            neighbour_rows = lax.dynamic_index_in_dim(masked, neighbour_index, 1, keepdims=False).astype(jnp.float32)
            part_y = jnp.einsum('ml,qlc->qmc', occupied[:, offset * BS:(offset + 1) * BS], neighbour_rows)
            y_acc = y_acc.at[:, :, offset * BS:(offset + neighbours) * BS].add(part_y)
        x_round = lax.optimization_barrier(x_acc.astype(jnp.bfloat16)).astype(jnp.float32)
        y_round = lax.optimization_barrier(y_acc.astype(jnp.bfloat16)).astype(jnp.float32)
        chi_sum = chi_sum + jnp.einsum('pmc,qmc->pq', x_round, y_round)
        return chi_sum, None

    chi, unused = lax.scan(one_block, jnp.zeros((ri_count, ri_count), jnp.float32),
                           jnp.arange(nblocks, dtype=jnp.int32))
    return chi
```

```python
import functools

import jax
import jax.numpy as jnp
from jax import lax
from jax.experimental import pallas as pl
from jax.experimental.pallas import tpu as pltpu
from jax.sharding import PartitionSpec as P

BS = 128
R = 2


def with_halo(array, sides, width):
    for axis, dim in sides:
        size, length = (lax.axis_size(axis), array.shape[dim])
        up = [(i, (i + 1) % size) for i in range(size)]
        down = [(j, i) for i, j in up]
        last = lax.slice_in_dim(array, length - width, length, axis=dim)
        initial = lax.slice_in_dim(array, 0, width, axis=dim)
        before = lax.ppermute(last, axis, up)
        after = lax.ppermute(initial, axis, down)
        array = jnp.concatenate([before, array, after], axis=dim)
    return array


def per_device(b_int, gv_band, go_band, mask):
    local = lax.all_to_all(b_int, "pair", split_axis=1, concat_axis=2, tiled=True)
    ri_count = local.shape[0]
    blocks_here = local.shape[1]
    neighbours = 2 * R + 1
    window = 4 * R + 1
    first_block = lax.axis_index("pair") * blocks_here
    own_mask = lax.dynamic_slice_in_dim(mask, first_block, blocks_here, 0)
    shaped = local.reshape(ri_count, blocks_here, BS, neighbours, BS)
    masked = (shaped * own_mask.astype(jnp.bfloat16)[None, :, None, :, None]).reshape(
        ri_count, blocks_here, BS, neighbours * BS
    )
    wide_three = with_halo(masked, (("pair", 1),), R)
    wide_virtual = with_halo(gv_band, (("pair", 0),), R)
    half_rows = go_band.shape[1]
    row_start = lax.axis_index("rep") * half_rows
    own_rows = lax.dynamic_slice_in_dim(masked, row_start, half_rows, 2)
    x_acc = jnp.zeros((ri_count, blocks_here, half_rows, window * BS), jnp.float32)
    y_acc = jnp.zeros((ri_count, blocks_here, half_rows, window * BS), jnp.float32)
    for offset in range(neighbours):
        x_acc = x_acc + jnp.einsum(
            "pimn,inc->pimc",
            own_rows[..., offset * BS : (offset + 1) * BS],
            wide_virtual[
                offset : offset + blocks_here, :, (2 * R - offset) * BS : (6 * R - offset + 1) * BS
            ],
            preferred_element_type=jnp.float32,
        )
        neighbour_rows = wide_three[:, offset : offset + blocks_here]
        part_y = jnp.einsum(
            "iml,qilc->qimc",
            go_band[:, :, offset * BS : (offset + 1) * BS],
            neighbour_rows,
            preferred_element_type=jnp.float32,
        )
        y_acc = y_acc.at[..., offset * BS : (offset + neighbours) * BS].add(part_y)
    x_flat = x_acc.astype(jnp.bfloat16).reshape(ri_count, -1)
    y_flat = y_acc.astype(jnp.bfloat16).reshape(ri_count, -1)
    product = jnp.einsum(
        "pk,qk->pq",
        x_flat,
        lax.all_gather(y_flat, "ri", axis=0, tiled=True),
        preferred_element_type=jnp.float32,
    )
    return lax.psum(product, ("pair", "rep"))


WINDOW = 4 * R + 1
NEAR = 2 * R + 1
TRIM = WINDOW + 1
VBAND = 6 * R + 1
MESH = pl.DeviceIdType.MESH


def remote(src, dst, send, recv, device):
    return pltpu.make_async_remote_copy(
        src_ref=src, dst_ref=dst, send_sem=send, recv_sem=recv, device_id=device, device_id_type=MESH
    )


def fused(
    n, b_ref, gv_ref, go_ref, mask_ref, out_ref,
    staged, three, halo, y_buf, x_buf, sums,
    m_local, m_send, m_recv, f_send, f_recv, y_send, y_recv, g_send, g_recv, h_send, h_recv, c_send, c_recv,
):
    z, x, r = lax.axis_index("pair"), lax.axis_index("ri"), lax.axis_index("rep")
    ri_here, nblk, rows, _ = b_ref.shape
    nb = gv_ref.shape[0]
    half = go_ref.shape[1]
    carried = ri_here // 2
    reach = nb + 2 * R
    sibling = {"rep": 1 - r}
    partner = {"ri": 1 - x}

    barrier = pltpu.get_barrier_semaphore()
    for d in range(n):
        other = lax.rem(z + d, n)
        if d:
            pl.semaphore_signal(barrier, inc=1, device_id={"pair": other}, device_id_type=MESH)
        pl.semaphore_signal(barrier, inc=1, device_id={"pair": other, "rep": 1 - r}, device_id_type=MESH)
    pl.semaphore_signal(barrier, inc=1, device_id=partner, device_id_type=MESH)

    for k in range(carried):
        for block in range(nblk):
            for o in range(NEAR):
                cols = slice(o * BS, (o + 1) * BS)
                present = mask_ref[block, o].astype(jnp.float32)
                value = (b_ref[carried * r + k, block, :, cols].astype(jnp.float32) * present).astype(jnp.bfloat16)
                staged[k, block, :, cols] = value
                if block < reach - R:
                    staged[k, block + nblk, :, cols] = value

    pl.semaphore_wait(barrier, 2 * n)

    def first(owner):
        return lax.rem(owner * nb + nblk - R, nblk)

    mine = pl.ds(pl.multiple_of(z * rows, rows), rows)
    for k in range(carried):
        q = carried * r + k
        for d in range(1, n):
            owner = lax.rem(z + d, n)
            remote(
                staged.at[k, pl.ds(first(owner), reach)], three.at[q, :, mine, :],
                m_send.at[k], m_recv.at[k], {"pair": owner},
            ).start()
        pltpu.make_async_copy(
            staged.at[k, pl.ds(first(z), reach)], three.at[q, :, mine, :], m_local.at[k]
        ).start()

    core_rows = pl.ds(pl.multiple_of(r * half, half), half)
    before = slice((VBAND - TRIM) * BS, VBAND * BS)
    after = slice(0, TRIM * BS)
    up, down = {"pair": lax.rem(z + 1, n)}, {"pair": lax.rem(z + n - 1, n)}
    virtual = [
        (gv_ref.at[nb - R : nb, core_rows, before], halo.at[0:R, core_rows, before], up),
        (gv_ref.at[0:R, core_rows, after], halo.at[R : 2 * R, core_rows, after], down),
    ]
    for s, (src, dst, device) in enumerate(virtual):
        remote(src, dst, g_send.at[s], g_recv.at[s], device).start()

    def occupied(q, slot):
        for i in range(nb):
            parts = [
                jnp.dot(
                    go_ref[i, :, o * BS : (o + 1) * BS], three[q, i + o], preferred_element_type=jnp.float32
                )
                for o in range(NEAR)
            ]
            for t in range(WINDOW):
                total = None
                for o in range(NEAR):
                    if 0 <= t - o < NEAR:
                        part = parts[o][:, (t - o) * BS : (t - o + 1) * BS]
                        total = part if total is None else total + part
                y_buf[0, i, q, :, t * BS : (t + 1) * BS] = total.astype(jnp.bfloat16)
        remote(y_buf.at[0, :, q], y_buf.at[1, :, q], y_send.at[slot], y_recv.at[slot], partner).start()

    for k in range(carried):
        q = carried * r + k
        theirs = carried * (1 - r) + k
        pltpu.make_async_copy(
            staged.at[k, pl.ds(first(z), reach)], three.at[q, :, mine, :], m_local.at[k]
        ).wait()
        others = three.at[q, :, 0 : (n - 1) * rows, :]
        remote(others, others, m_send.at[k], m_recv.at[k], sibling).wait_recv()
        remote(three.at[q], three.at[q], f_send.at[k], f_recv.at[k], sibling).start()
        occupied(q, 2 * k)
        remote(three.at[theirs], three.at[theirs], f_send.at[k], f_recv.at[k], sibling).wait_recv()
        occupied(theirs, 2 * k + 1)

    for s, (src, dst, device) in enumerate(virtual):
        remote(dst, dst, g_send.at[s], g_recv.at[s], sibling).wait_recv()
        remote(dst, dst, h_send.at[s], h_recv.at[s], sibling).start()
    for s, (src, dst, device) in enumerate(virtual):
        remote(dst, dst, h_send.at[s], h_recv.at[s], sibling).wait_recv()

    def virtual_rows(j, cols):
        if j < R:
            return halo[j, :, cols]
        if j < R + nb:
            return gv_ref[j - R, :, cols]
        return halo[j - nb, :, cols]

    def products(side):
        total = None
        for i in range(nb):
            part = lax.dot_general(
                x_buf[i], y_buf[side, i].reshape(ri_here * half, WINDOW * BS),
                (((1,), (1,)), ((), ())), preferred_element_type=jnp.float32,
            )
            total = part if total is None else total + part
        return total

    for i in range(nb):
        total = None
        for o in range(NEAR):
            left = three[:, i + R, core_rows, o * BS : (o + 1) * BS].reshape(ri_here * half, BS)
            part = jnp.dot(
                left, virtual_rows(i + o, slice((2 * R - o) * BS, (6 * R - o + 1) * BS)),
                preferred_element_type=jnp.float32,
            )
            total = part if total is None else total + part
        x_buf[i] = total.astype(jnp.bfloat16)

    size = ri_here * half
    row_id = lax.broadcasted_iota(jnp.int32, (size, size), 0)
    col_id = lax.broadcasted_iota(jnp.int32, (size, size), 1)
    same = lax.rem(row_id, half) == lax.rem(col_id, half)
    col_of = lax.broadcasted_iota(jnp.int32, (ri_here, size), 1) // half
    lane = lax.broadcasted_iota(jnp.int32, (ri_here, BS), 1)
    result = jnp.zeros((ri_here, BS), jnp.float32)
    for side in range(2):
        if side:
            for slot in range(ri_here):
                q = carried * (r if slot % 2 == 0 else 1 - r) + slot // 2
                landed = y_buf.at[1, :, q]
                remote(landed, landed, y_send.at[slot], y_recv.at[slot], partner).wait_recv()
        diagonal = jnp.where(same, products(side), 0.0).reshape(ri_here, half, size).sum(axis=1)
        base = ri_here * (x if side == 0 else 1 - x)
        for q in range(ri_here):
            value = jnp.sum(jnp.where(col_of == q, diagonal, 0.0), axis=1, keepdims=True)
            result = jnp.where(lane == base + q, value, result)

    slot = 2 * z + r
    sums[slot, 0:ri_here, :] = result
    for d in range(n):
        other = lax.rem(z + d, n)
        if d:
            remote(sums.at[slot], sums.at[slot], c_send, c_recv, {"pair": other}).start()
        remote(sums.at[slot], sums.at[slot], c_send, c_recv, {"pair": other, "rep": 1 - r}).start()
    seven = sums.at[0 : 2 * n - 1]
    remote(seven, seven, c_send, c_recv, sibling).wait_recv()
    total = sums[0]
    for s in range(1, 2 * n):
        total = total + sums[s]
    out_ref[...] = total[0:ri_here, 0 : 2 * ri_here]

    remote(seven, seven, c_send, c_recv, sibling).wait_send()
    for k in range(carried):
        q = carried * r + k
        others = three.at[q, :, 0 : (n - 1) * rows, :]
        remote(others, others, m_send.at[k], m_recv.at[k], sibling).wait_send()
        remote(three.at[q], three.at[q], f_send.at[k], f_recv.at[k], sibling).wait_send()
    for slot in range(ri_here):
        q = carried * (r if slot % 2 == 0 else 1 - r) + slot // 2
        remote(y_buf.at[0, :, q], y_buf.at[0, :, q], y_send.at[slot], y_recv.at[slot], partner).wait_send()
    for s, (src, dst, device) in enumerate(virtual):
        remote(src, dst, g_send.at[s], g_recv.at[s], device).wait_send()
        remote(dst, dst, h_send.at[s], h_recv.at[s], sibling).wait_send()


def one_kernel(b_int, gv_band, go_band, mask):
    n = lax.axis_size("pair")
    ri_here, nblk, rows, width = b_int.shape
    nb = gv_band.shape[0]
    half = go_band.shape[1]
    carried = ri_here // 2
    reach = nb + 2 * R
    dma = pltpu.SemaphoreType.DMA
    vmem = pl.BlockSpec(memory_space=pltpu.VMEM)
    return pl.pallas_call(
        functools.partial(fused, n),
        out_shape=jax.ShapeDtypeStruct((ri_here, 2 * ri_here), jnp.float32),
        in_specs=[vmem, vmem, vmem, pl.BlockSpec(memory_space=pltpu.SMEM)],
        out_specs=vmem,
        scratch_shapes=[
            pltpu.VMEM((carried, nblk + reach - R, rows, width), jnp.bfloat16),
            pltpu.VMEM((ri_here, reach, BS, width), jnp.bfloat16),
            pltpu.VMEM((2 * R, BS, gv_band.shape[2]), jnp.bfloat16),
            pltpu.VMEM((2, nb, ri_here, half, WINDOW * BS), jnp.bfloat16),
            pltpu.VMEM((nb, ri_here * half, WINDOW * BS), jnp.bfloat16),
            pltpu.VMEM((2 * n, 8, BS), jnp.float32),
            dma((carried,)), dma((carried,)), dma((carried,)), dma((carried,)), dma((carried,)),
            dma((ri_here,)), dma((ri_here,)), dma((2,)), dma((2,)), dma((2,)), dma((2,)), dma, dma,
        ],
        compiler_params=pltpu.CompilerParams(
            collective_id=0, has_side_effects=True, vmem_limit_bytes=40 * 1024 * 1024
        ),
    )(b_int, gv_band, go_band, mask)


def on_device(b_int, gv_band, go_band, mask):
    fits = (
        lax.axis_size("ri") == 2
        and lax.axis_size("rep") == 2
        and b_int.shape[2] % 16 == 0
        and b_int.shape[0] in (2, 4, 8)
        and gv_band.shape[0] >= R
        and gv_band.shape[0] + R <= b_int.shape[1]
    )
    return (one_kernel if fits else per_device)(b_int, gv_band, go_band, mask)


def solution(mesh):
    in_specs = (
        P(("groups", "ri"), None, "pair", None),
        P(("groups", "pair"), None, None),
        P(("groups", "pair"), "rep", None),
        P("groups", None),
    )
    out_specs = P(("groups", "ri"), None)
    return jax.shard_map(
        on_device, mesh=mesh, in_specs=in_specs, out_specs=out_specs, check_vma=False
    )
```

```python
import functools

import jax
import jax.numpy as jnp
from jax import lax
from jax.experimental import pallas as pl
from jax.experimental.pallas import tpu as pltpu
from jax.sharding import PartitionSpec as P

BS = 128
R = 2


def with_halo(array, sides, width):
    for axis, dim in sides:
        size, length = (lax.axis_size(axis), array.shape[dim])
        up = [(i, (i + 1) % size) for i in range(size)]
        down = [(j, i) for i, j in up]
        last = lax.slice_in_dim(array, length - width, length, axis=dim)
        initial = lax.slice_in_dim(array, 0, width, axis=dim)
        before = lax.ppermute(last, axis, up)
        after = lax.ppermute(initial, axis, down)
        array = jnp.concatenate([before, array, after], axis=dim)
    return array


def per_device(b_int, gv_band, go_band, mask):
    local = lax.all_to_all(b_int, "pair", split_axis=1, concat_axis=2, tiled=True)
    ri_count = local.shape[0]
    blocks_here = local.shape[1]
    neighbours = 2 * R + 1
    window = 4 * R + 1
    first_block = lax.axis_index("pair") * blocks_here
    own_mask = lax.dynamic_slice_in_dim(mask, first_block, blocks_here, 0)
    shaped = local.reshape(ri_count, blocks_here, BS, neighbours, BS)
    masked = (shaped * own_mask.astype(jnp.bfloat16)[None, :, None, :, None]).reshape(
        ri_count, blocks_here, BS, neighbours * BS
    )
    wide_three = with_halo(masked, (("pair", 1),), R)
    wide_virtual = with_halo(gv_band, (("pair", 0),), R)
    half_rows = go_band.shape[1]
    row_start = lax.axis_index("rep") * half_rows
    own_rows = lax.dynamic_slice_in_dim(masked, row_start, half_rows, 2)
    x_acc = jnp.zeros((ri_count, blocks_here, half_rows, window * BS), jnp.float32)
    y_acc = jnp.zeros((ri_count, blocks_here, half_rows, window * BS), jnp.float32)
    for offset in range(neighbours):
        x_acc = x_acc + jnp.einsum(
            "pimn,inc->pimc",
            own_rows[..., offset * BS : (offset + 1) * BS],
            wide_virtual[
                offset : offset + blocks_here, :, (2 * R - offset) * BS : (6 * R - offset + 1) * BS
            ],
            preferred_element_type=jnp.float32,
        )
        neighbour_rows = wide_three[:, offset : offset + blocks_here]
        part_y = jnp.einsum(
            "iml,qilc->qimc",
            go_band[:, :, offset * BS : (offset + 1) * BS],
            neighbour_rows,
            preferred_element_type=jnp.float32,
        )
        y_acc = y_acc.at[..., offset * BS : (offset + neighbours) * BS].add(part_y)
    x_flat = x_acc.astype(jnp.bfloat16).reshape(ri_count, -1)
    y_flat = y_acc.astype(jnp.bfloat16).reshape(ri_count, -1)
    product = jnp.einsum(
        "pk,qk->pq",
        x_flat,
        lax.all_gather(y_flat, "ri", axis=0, tiled=True),
        preferred_element_type=jnp.float32,
    )
    return lax.psum(product, ("pair", "rep"))


WINDOW = 4 * R + 1
NEAR = 2 * R + 1
TRIM = WINDOW + 1
VBAND = 6 * R + 1
MESH = pl.DeviceIdType.MESH


def remote(src, dst, send, recv, device):
    return pltpu.make_async_remote_copy(
        src_ref=src, dst_ref=dst, send_sem=send, recv_sem=recv, device_id=device, device_id_type=MESH
    )


def fused(
    n, b_ref, gv_ref, go_ref, mask_ref, out_ref,
    three, virtual, occ, present, y_buf, x_buf, sums,
    in_sem, own_sem, right_send, right_recv, left_send, left_recv, f_send, f_recv,
    y_send, y_recv, g_send, g_recv, h_send, h_recv, c_send, c_recv,
):
    z, x, r = lax.axis_index("pair"), lax.axis_index("ri"), lax.axis_index("rep")
    ri_here, nblk, rows, width = b_ref.shape
    nb = gv_ref.shape[0]
    half = go_ref.shape[1]
    reach = nb + 2 * R
    part_rows = rows // 2
    sibling = {"rep": 1 - r}
    partner = {"ri": 1 - x}

    barrier = pltpu.get_barrier_semaphore()
    for d in range(n):
        other = lax.rem(z + d, n)
        if d:
            pl.semaphore_signal(barrier, inc=1, device_id={"pair": other}, device_id_type=MESH)
        pl.semaphore_signal(barrier, inc=1, device_id={"pair": other, "rep": 1 - r}, device_id_type=MESH)
    pl.semaphore_signal(barrier, inc=1, device_id=partner, device_id_type=MESH)

    loads = [
        pltpu.make_async_copy(gv_ref, virtual.at[R : R + nb], in_sem.at[0]),
        pltpu.make_async_copy(go_ref, occ, in_sem.at[1]),
        pltpu.make_async_copy(mask_ref, present, in_sem.at[2]),
    ]
    for load in loads:
        load.start()

    def at_each(step):
        for place in range(n):
            pl.when(z == place)(functools.partial(step, place))

    def needed(place):
        low, high = place * nb - R, place * nb + nb + R
        if low < 0:
            return [(0, high), (nblk + low, -low)]
        if high > nblk:
            return [(0, high - nblk), (low, nblk - low)]
        return [(low, high - low)]

    def from_left(place):
        low = max(place * nb - R, R)
        return [(0, R), (low, nblk - low)]

    def from_right(place):
        high = min(place * nb + nb + R, nblk - R)
        return [(0, high), (nblk - R, R)]

    def count(runs):
        return sum(size for _, size in runs)

    core_part = pl.ds(pl.multiple_of(r * part_rows, part_rows), part_rows)

    def own(q, place):
        return [
            pltpu.make_async_copy(b_ref.at[q, pl.ds(a, m)], three.at[q, pl.ds(a, m), place], own_sem.at[q])
            for a, m in needed(place)
        ]

    def send(q, hop, place):
        for source, to, runs, sems in (
            (place - hop, place + 1, from_left, (right_send, right_recv)),
            (place + hop, place - 1, from_right, (left_send, left_recv)),
        ):
            if 0 <= source < n and 0 <= to < n:
                for a, m in runs(to):
                    dst = three.at[q, pl.ds(a, m), source, core_part]
                    src = b_ref.at[q, pl.ds(a, m), core_part] if hop == 0 else dst
                    remote(src, dst, sems[0].at[q, hop], sems[1].at[q, hop], {"pair": to}).start()

    def sent(q, hop, place):
        for source, to, runs, sems in (
            (place - hop, place + 1, from_left, (right_send, right_recv)),
            (place + hop, place - 1, from_right, (left_send, left_recv)),
        ):
            if 0 <= source < n and 0 <= to < n:
                ref = three.at[q, pl.ds(0, count(runs(to))), source, core_part]
                remote(ref, ref, sems[0].at[q, hop], sems[1].at[q, hop], sibling).wait_send()

    def arrived(q, hop, place):
        for source, runs, sems in (
            (place - 1 - hop, from_left, (right_send, right_recv)),
            (place + 1 + hop, from_right, (left_send, left_recv)),
        ):
            if 0 <= source < n:
                ref = three.at[q, pl.ds(0, count(runs(place))), source, core_part]
                remote(ref, ref, sems[0].at[q, hop], sems[1].at[q, hop], sibling).wait_recv()

    def share(q, hop, place):
        for source in (place - 1 - hop, place + 1 + hop):
            if 0 <= source < n:
                for a, m in needed(place):
                    ref = three.at[q, pl.ds(a, m), source, core_part]
                    remote(ref, ref, f_send.at[q], f_recv.at[q], sibling).start()

    def first_sends(place):
        for q in range(ri_here):
            for copy in own(q, place):
                copy.start()

    pl.semaphore_wait(barrier, 2 * n)
    at_each(functools.partial(send, 0, 0))
    at_each(functools.partial(send, 1, 0))
    at_each(first_sends)

    core_rows = pl.ds(pl.multiple_of(r * half, half), half)
    wide, narrow = TRIM * BS, WINDOW * BS
    last = VBAND * BS
    up, down = {"pair": lax.rem(z + 1, n)}, {"pair": lax.rem(z + n - 1, n)}
    halos = [
        (gv_ref.at[nb - R : nb, core_rows, last - wide : last], virtual.at[0:R, core_rows, last - wide : last], up),
        (gv_ref.at[0:R, core_rows, 0:wide], virtual.at[nb + R : reach, core_rows, 0:wide], down),
    ]

    def block_of(j):
        return lax.rem(z * nb + (nblk - R + j), nblk)

    def occupied(q):
        for i in range(nb):
            parts = []
            for o in range(NEAR):
                block = block_of(i + o)
                part = jnp.dot(
                    occ[i, :, o * BS : (o + 1) * BS], three[q, block].reshape(n * rows, width),
                    preferred_element_type=jnp.float32,
                )
                parts.append([
                    part[:, p * BS : (p + 1) * BS] * present[p, block].astype(jnp.float32) for p in range(NEAR)
                ])
            for t in range(WINDOW):
                total = None
                for o in range(NEAR):
                    if 0 <= t - o < NEAR:
                        part = parts[o][t - o]
                        total = part if total is None else total + part
                y_buf[0, i, q, :, t * BS : (t + 1) * BS] = total.astype(jnp.bfloat16)
        remote(y_buf.at[0, :, q], y_buf.at[1, :, q], y_send.at[q], y_recv.at[q], partner).start()

    for load in loads:
        load.wait()
    def pass_on(q, hop, place):
        arrived(q, hop, place)
        if hop + 1 < n - 1:
            send(q, hop + 1, place)
        if hop == 0 and q + 2 < ri_here:
            send(q + 2, 0, place)
        share(q, hop, place)

    def response(q):
        own_ref = three.at[q, pl.ds(0, reach), 0]
        pltpu.make_async_copy(own_ref, own_ref, own_sem.at[q]).wait()
        shared = three.at[q, pl.ds(0, reach), pl.ds(0, n - 1), core_part]
        remote(shared, shared, f_send.at[q], f_recv.at[q], sibling).wait_recv()
        occupied(q)

    seen = set()

    def visit(q, hop):
        if (q, hop) not in seen and q < ri_here and hop < n - 1:
            seen.add((q, hop))
            at_each(functools.partial(pass_on, q, hop))

    for q in range(ri_here):
        for hop in range(n - 1):
            if hop == n - 2:
                visit(q + 1, 0)
                if q == ri_here - 1:
                    for s, (src, dst, device) in enumerate(halos):
                        remote(src, dst, g_send.at[s], g_recv.at[s], device).start()
            visit(q, hop)
        response(q)

    for s, (src, dst, device) in enumerate(halos):
        remote(dst, dst, g_send.at[s], g_recv.at[s], sibling).wait_recv()
        remote(dst, dst, h_send.at[s], h_recv.at[s], sibling).start()
    for s, (src, dst, device) in enumerate(halos):
        remote(dst, dst, h_send.at[s], h_recv.at[s], sibling).wait_recv()

    def products(side):
        total = None
        for i in range(nb):
            part = lax.dot_general(
                x_buf[i], y_buf[side, i].reshape(ri_here * half, WINDOW * BS),
                (((1,), (1,)), ((), ())), preferred_element_type=jnp.float32,
            )
            total = part if total is None else total + part
        return total

    owners = half // rows
    for i in range(nb):
        total = None
        block = z * nb + i
        for o in range(NEAR):
            left = three[:, block, pl.ds(r * owners, owners), :, o * BS : (o + 1) * BS].reshape(ri_here * half, BS)
            part = jnp.dot(
                left, virtual[i + o, :, (2 * R - o) * BS : (6 * R - o + 1) * BS],
                preferred_element_type=jnp.float32,
            ) * present[o, block].astype(jnp.float32)
            total = part if total is None else total + part
        x_buf[i] = total.astype(jnp.bfloat16)

    size = ri_here * half
    row_id = lax.broadcasted_iota(jnp.int32, (size, size), 0)
    col_id = lax.broadcasted_iota(jnp.int32, (size, size), 1)
    same = lax.rem(row_id, half) == lax.rem(col_id, half)
    col_of = lax.broadcasted_iota(jnp.int32, (ri_here, size), 1) // half
    lane = lax.broadcasted_iota(jnp.int32, (ri_here, BS), 1)
    result = jnp.zeros((ri_here, BS), jnp.float32)
    for side in range(2):
        if side:
            for q in range(ri_here):
                landed = y_buf.at[1, :, q]
                remote(landed, landed, y_send.at[q], y_recv.at[q], partner).wait_recv()
        diagonal = jnp.where(same, products(side), 0.0).reshape(ri_here, half, size).sum(axis=1)
        base = ri_here * (x if side == 0 else 1 - x)
        for q in range(ri_here):
            value = jnp.sum(jnp.where(col_of == q, diagonal, 0.0), axis=1, keepdims=True)
            result = jnp.where(lane == base + q, value, result)

    slot = 2 * z + r
    sums[slot, 0:ri_here, :] = result
    for d in range(n):
        other = lax.rem(z + d, n)
        if d:
            remote(sums.at[slot], sums.at[slot], c_send, c_recv, {"pair": other}).start()
        remote(sums.at[slot], sums.at[slot], c_send, c_recv, {"pair": other, "rep": 1 - r}).start()
    seven = sums.at[0 : 2 * n - 1]
    remote(seven, seven, c_send, c_recv, sibling).wait_recv()
    total = sums[0]
    for s in range(1, 2 * n):
        total = total + sums[s]
    out_ref[...] = total[0:ri_here, 0 : 2 * ri_here]

    remote(seven, seven, c_send, c_recv, sibling).wait_send()
    for q in range(ri_here):
        for hop in range(n - 1):
            at_each(functools.partial(sent, q, hop))
        shared = three.at[q, pl.ds(0, reach), pl.ds(0, n - 1), core_part]
        remote(shared, shared, f_send.at[q], f_recv.at[q], sibling).wait_send()
        remote(y_buf.at[0, :, q], y_buf.at[0, :, q], y_send.at[q], y_recv.at[q], partner).wait_send()
    for s, (src, dst, device) in enumerate(halos):
        remote(src, dst, g_send.at[s], g_recv.at[s], device).wait_send()
        remote(dst, dst, h_send.at[s], h_recv.at[s], sibling).wait_send()


def one_kernel(b_int, gv_band, go_band, mask):
    n = lax.axis_size("pair")
    ri_here, nblk, rows, width = b_int.shape
    nb = gv_band.shape[0]
    half = go_band.shape[1]
    dma = pltpu.SemaphoreType.DMA
    hbm = pl.BlockSpec(memory_space=pltpu.HBM)
    per_hop, per_q = dma((ri_here, n - 1)), dma((ri_here,))
    return pl.pallas_call(
        functools.partial(fused, n),
        out_shape=jax.ShapeDtypeStruct((ri_here, 2 * ri_here), jnp.float32),
        in_specs=[hbm, hbm, hbm, hbm],
        out_specs=pl.BlockSpec(memory_space=pltpu.VMEM),
        scratch_shapes=[
            pltpu.VMEM((ri_here, nblk, n, rows, width), jnp.bfloat16),
            pltpu.VMEM((nb + 2 * R, BS, gv_band.shape[2]), jnp.bfloat16),
            pltpu.VMEM(go_band.shape, jnp.bfloat16),
            pltpu.SMEM(mask.shape[::-1], jnp.int32),
            pltpu.VMEM((2, nb, ri_here, half, WINDOW * BS), jnp.bfloat16),
            pltpu.VMEM((nb, ri_here * half, WINDOW * BS), jnp.bfloat16),
            pltpu.VMEM((2 * n, 8, BS), jnp.float32),
            dma((3,)), per_q, per_hop, per_hop, per_hop, per_hop, per_q, per_q,
            per_q, per_q, dma((2,)), dma((2,)), dma((2,)), dma((2,)), dma, dma,
        ],
        compiler_params=pltpu.CompilerParams(
            collective_id=0, has_side_effects=True, vmem_limit_bytes=63 * 1024 * 1024
        ),
    )(b_int, gv_band, go_band, mask.T)


def on_device(b_int, gv_band, go_band, mask):
    fits = (
        lax.axis_size("ri") == 2
        and lax.axis_size("rep") == 2
        and 2 <= lax.axis_size("pair") <= 4
        and b_int.shape[2] % 32 == 0
        and go_band.shape[1] % b_int.shape[2] == 0
        and b_int.shape[0] in (2, 4, 8)
        and gv_band.shape[0] >= R
        and gv_band.shape[0] + 2 * R <= b_int.shape[1]
    )
    return (one_kernel if fits else per_device)(b_int, gv_band, go_band, mask)


def solution(mesh):
    in_specs = (
        P(("groups", "ri"), None, "pair", None),
        P(("groups", "pair"), None, None),
        P(("groups", "pair"), "rep", None),
        P("groups", None),
    )
    out_specs = P(("groups", "ri"), None)
    return jax.shard_map(
        on_device, mesh=mesh, in_specs=in_specs, out_specs=out_specs, check_vma=False
    )
```

```python
import functools

import jax
import jax.numpy as jnp
from jax import lax
from jax.experimental import pallas as pl
from jax.experimental.pallas import tpu as pltpu
from jax.sharding import PartitionSpec as P

BS = 128
R = 2


def with_halo(array, sides, width):
    for axis, dim in sides:
        size, length = (lax.axis_size(axis), array.shape[dim])
        up = [(i, (i + 1) % size) for i in range(size)]
        down = [(j, i) for i, j in up]
        last = lax.slice_in_dim(array, length - width, length, axis=dim)
        initial = lax.slice_in_dim(array, 0, width, axis=dim)
        before = lax.ppermute(last, axis, up)
        after = lax.ppermute(initial, axis, down)
        array = jnp.concatenate([before, array, after], axis=dim)
    return array


def per_device(b_int, gv_band, go_band, mask):
    local = lax.all_to_all(b_int, "pair", split_axis=1, concat_axis=2, tiled=True)
    ri_count = local.shape[0]
    blocks_here = local.shape[1]
    neighbours = 2 * R + 1
    window = 4 * R + 1
    first_block = lax.axis_index("pair") * blocks_here
    own_mask = lax.dynamic_slice_in_dim(mask, first_block, blocks_here, 0)
    shaped = local.reshape(ri_count, blocks_here, BS, neighbours, BS)
    masked = (shaped * own_mask.astype(jnp.bfloat16)[None, :, None, :, None]).reshape(
        ri_count, blocks_here, BS, neighbours * BS
    )
    wide_three = with_halo(masked, (("pair", 1),), R)
    wide_virtual = with_halo(gv_band, (("pair", 0),), R)
    half_rows = go_band.shape[1]
    row_start = lax.axis_index("rep") * half_rows
    own_rows = lax.dynamic_slice_in_dim(masked, row_start, half_rows, 2)
    x_acc = jnp.zeros((ri_count, blocks_here, half_rows, window * BS), jnp.float32)
    y_acc = jnp.zeros((ri_count, blocks_here, half_rows, window * BS), jnp.float32)
    for offset in range(neighbours):
        x_acc = x_acc + jnp.einsum(
            "pimn,inc->pimc",
            own_rows[..., offset * BS : (offset + 1) * BS],
            wide_virtual[
                offset : offset + blocks_here, :, (2 * R - offset) * BS : (6 * R - offset + 1) * BS
            ],
            preferred_element_type=jnp.float32,
        )
        neighbour_rows = wide_three[:, offset : offset + blocks_here]
        part_y = jnp.einsum(
            "iml,qilc->qimc",
            go_band[:, :, offset * BS : (offset + 1) * BS],
            neighbour_rows,
            preferred_element_type=jnp.float32,
        )
        y_acc = y_acc.at[..., offset * BS : (offset + neighbours) * BS].add(part_y)
    x_flat = x_acc.astype(jnp.bfloat16).reshape(ri_count, -1)
    y_flat = y_acc.astype(jnp.bfloat16).reshape(ri_count, -1)
    product = jnp.einsum(
        "pk,qk->pq",
        x_flat,
        lax.all_gather(y_flat, "ri", axis=0, tiled=True),
        preferred_element_type=jnp.float32,
    )
    return lax.psum(product, ("pair", "rep"))


WINDOW = 4 * R + 1
NEAR = 2 * R + 1
TRIM = WINDOW + 1
VBAND = 6 * R + 1
MESH = pl.DeviceIdType.MESH


def remote(src, dst, send, recv, device):
    return pltpu.make_async_remote_copy(
        src_ref=src, dst_ref=dst, send_sem=send, recv_sem=recv, device_id=device, device_id_type=MESH
    )


def fused(
    n, b_ref, gv_ref, go_ref, mask_ref, out_ref,
    three, virtual, occ, present, y_buf, x_acc, x_buf, sums,
    in_sem, own_sem, right_send, right_recv, left_send, left_recv, f_send, f_recv,
    y_send, y_recv, g_send, g_recv, h_send, h_recv, c_send, c_recv,
):
    z, x, r = lax.axis_index("pair"), lax.axis_index("ri"), lax.axis_index("rep")
    ri_here, nblk, rows, width = b_ref.shape
    nb = gv_ref.shape[0]
    half = go_ref.shape[1]
    reach = nb + 2 * R
    part_rows = rows // 2
    sibling = {"rep": 1 - r}
    partner = {"ri": 1 - x}

    barrier = pltpu.get_barrier_semaphore()
    for d in range(n):
        other = lax.rem(z + d, n)
        if d:
            pl.semaphore_signal(barrier, inc=1, device_id={"pair": other}, device_id_type=MESH)
        pl.semaphore_signal(barrier, inc=1, device_id={"pair": other, "rep": 1 - r}, device_id_type=MESH)
    pl.semaphore_signal(barrier, inc=1, device_id=partner, device_id_type=MESH)

    loads = [
        pltpu.make_async_copy(gv_ref, virtual.at[R : R + nb], in_sem.at[0]),
        pltpu.make_async_copy(go_ref, occ, in_sem.at[1]),
        pltpu.make_async_copy(mask_ref, present, in_sem.at[2]),
    ]
    for load in loads:
        load.start()

    def at_each(step):
        for place in range(n):
            pl.when(z == place)(functools.partial(step, place))

    def needed(place):
        low, high = place * nb - R, place * nb + nb + R
        if low < 0:
            return [(0, high), (nblk + low, -low)]
        if high > nblk:
            return [(0, high - nblk), (low, nblk - low)]
        return [(low, high - low)]

    def from_left(place):
        low = max(place * nb - R, R)
        return [(0, R), (low, nblk - low)]

    def from_right(place):
        high = min(place * nb + nb + R, nblk - R)
        return [(0, high), (nblk - R, R)]

    def count(runs):
        return sum(size for _, size in runs)

    core_part = pl.ds(pl.multiple_of(r * part_rows, part_rows), part_rows)

    def own(q, place):
        return [
            pltpu.make_async_copy(b_ref.at[q, pl.ds(a, m)], three.at[q, pl.ds(a, m), place], own_sem.at[q])
            for a, m in needed(place)
        ]

    def send(q, hop, place):
        for source, to, runs, sems in (
            (place - hop, place + 1, from_left, (right_send, right_recv)),
            (place + hop, place - 1, from_right, (left_send, left_recv)),
        ):
            if 0 <= source < n and 0 <= to < n:
                for a, m in runs(to):
                    dst = three.at[q, pl.ds(a, m), source, core_part]
                    src = b_ref.at[q, pl.ds(a, m), core_part] if hop == 0 else dst
                    remote(src, dst, sems[0].at[q, hop], sems[1].at[q, hop], {"pair": to}).start()

    def sent(q, hop, place):
        for source, to, runs, sems in (
            (place - hop, place + 1, from_left, (right_send, right_recv)),
            (place + hop, place - 1, from_right, (left_send, left_recv)),
        ):
            if 0 <= source < n and 0 <= to < n:
                ref = three.at[q, pl.ds(0, count(runs(to))), source, core_part]
                remote(ref, ref, sems[0].at[q, hop], sems[1].at[q, hop], sibling).wait_send()

    def arrived(q, hop, place):
        for source, runs, sems in (
            (place - 1 - hop, from_left, (right_send, right_recv)),
            (place + 1 + hop, from_right, (left_send, left_recv)),
        ):
            if 0 <= source < n:
                ref = three.at[q, pl.ds(0, count(runs(place))), source, core_part]
                remote(ref, ref, sems[0].at[q, hop], sems[1].at[q, hop], sibling).wait_recv()

    def share(q, hop, place):
        for source in (place - 1 - hop, place + 1 + hop):
            if 0 <= source < n:
                for a, m in needed(place):
                    ref = three.at[q, pl.ds(a, m), source, core_part]
                    remote(ref, ref, f_send.at[q], f_recv.at[q], sibling).start()

    def first_sends(place):
        for q in range(ri_here):
            for copy in own(q, place):
                copy.start()

    pl.semaphore_wait(barrier, 2 * n)
    at_each(functools.partial(send, 0, 0))
    at_each(functools.partial(send, 1, 0))
    at_each(first_sends)

    core_rows = pl.ds(pl.multiple_of(r * half, half), half)
    wide, narrow = TRIM * BS, WINDOW * BS
    last = VBAND * BS
    up, down = {"pair": lax.rem(z + 1, n)}, {"pair": lax.rem(z + n - 1, n)}
    halos = [
        (gv_ref.at[nb - R : nb, core_rows, last - wide : last], virtual.at[0:R, core_rows, last - wide : last], up),
        (gv_ref.at[0:R, core_rows, 0:wide], virtual.at[nb + R : reach, core_rows, 0:wide], down),
    ]

    def block_of(j):
        return lax.rem(z * nb + (nblk - R + j), nblk)

    def occupied(q):
        for i in range(nb):
            parts = []
            for o in range(NEAR):
                block = block_of(i + o)
                part = jnp.dot(
                    occ[i, :, o * BS : (o + 1) * BS], three[q, block].reshape(n * rows, width),
                    preferred_element_type=jnp.float32,
                )
                parts.append([
                    part[:, p * BS : (p + 1) * BS] * present[p, block].astype(jnp.float32) for p in range(NEAR)
                ])
            for t in range(WINDOW):
                total = None
                for o in range(NEAR):
                    if 0 <= t - o < NEAR:
                        part = parts[o][t - o]
                        total = part if total is None else total + part
                y_buf[0, i, q, :, t * BS : (t + 1) * BS] = total.astype(jnp.bfloat16)
            remote(y_buf.at[0, i, q], y_buf.at[1, i, q], y_send.at[q], y_recv.at[q], partner).start()

    for load in loads:
        load.wait()
    def pass_on(q, hop, place):
        arrived(q, hop, place)
        if hop + 1 < n - 1:
            send(q, hop + 1, place)
        if hop == 0 and q + 2 < ri_here:
            send(q + 2, 0, place)
        share(q, hop, place)

    def response(q):
        own_ref = three.at[q, pl.ds(0, reach), 0]
        pltpu.make_async_copy(own_ref, own_ref, own_sem.at[q]).wait()
        shared = three.at[q, pl.ds(0, reach), pl.ds(0, n - 1), core_part]
        remote(shared, shared, f_send.at[q], f_recv.at[q], sibling).wait_recv()
        occupied(q)

    seen = set()

    def visit(q, hop):
        if (q, hop) not in seen and q < ri_here and hop < n - 1:
            seen.add((q, hop))
            at_each(functools.partial(pass_on, q, hop))

    for q in range(ri_here):
        for hop in range(n - 1):
            if hop == n - 2:
                visit(q + 1, 0)
                if q == ri_here - 1:
                    for s, (src, dst, device) in enumerate(halos):
                        remote(src, dst, g_send.at[s], g_recv.at[s], device).start()
            visit(q, hop)
        response(q)

    owners = half // rows

    def virtual_products(i, offsets):
        total = None
        block = z * nb + i
        for o in offsets:
            left = three[:, block, pl.ds(r * owners, owners), :, o * BS : (o + 1) * BS].reshape(ri_here * half, BS)
            part = jnp.dot(
                left, virtual[i + o, :, (2 * R - o) * BS : (6 * R - o + 1) * BS],
                preferred_element_type=jnp.float32,
            ) * present[o, block].astype(jnp.float32)
            total = part if total is None else total + part
        return total

    def here(i, o):
        return R <= i + o < R + nb

    for i in range(nb):
        x_acc[i] = virtual_products(i, [o for o in range(NEAR) if here(i, o)])

    for s, (src, dst, device) in enumerate(halos):
        remote(dst, dst, g_send.at[s], g_recv.at[s], sibling).wait_recv()
        remote(dst, dst, h_send.at[s], h_recv.at[s], sibling).start()
    for s, (src, dst, device) in enumerate(halos):
        remote(dst, dst, h_send.at[s], h_recv.at[s], sibling).wait_recv()

    def products(side):
        total = None
        for i in range(nb):
            part = lax.dot_general(
                x_buf[i], y_buf[side, i].reshape(ri_here * half, WINDOW * BS),
                (((1,), (1,)), ((), ())), preferred_element_type=jnp.float32,
            )
            total = part if total is None else total + part
        return total

    for i in range(nb):
        total = x_acc[i]
        if not all(here(i, o) for o in range(NEAR)):
            total = total + virtual_products(i, [o for o in range(NEAR) if not here(i, o)])
        x_buf[i] = total.astype(jnp.bfloat16)

    size = ri_here * half
    row_id = lax.broadcasted_iota(jnp.int32, (size, size), 0)
    col_id = lax.broadcasted_iota(jnp.int32, (size, size), 1)
    same = lax.rem(row_id, half) == lax.rem(col_id, half)
    col_of = lax.broadcasted_iota(jnp.int32, (ri_here, size), 1) // half
    lane = lax.broadcasted_iota(jnp.int32, (ri_here, BS), 1)
    result = jnp.zeros((ri_here, BS), jnp.float32)
    for side in range(2):
        if side:
            for q in range(ri_here):
                landed = y_buf.at[1, :, q]
                remote(landed, landed, y_send.at[q], y_recv.at[q], partner).wait_recv()
        diagonal = jnp.where(same, products(side), 0.0).reshape(ri_here, half, size).sum(axis=1)
        base = ri_here * (x if side == 0 else 1 - x)
        for q in range(ri_here):
            value = jnp.sum(jnp.where(col_of == q, diagonal, 0.0), axis=1, keepdims=True)
            result = jnp.where(lane == base + q, value, result)

    slot = 2 * z + r
    sums[slot, 0:ri_here, :] = result
    for d in range(n):
        other = lax.rem(z + d, n)
        if d:
            remote(sums.at[slot], sums.at[slot], c_send, c_recv, {"pair": other}).start()
        remote(sums.at[slot], sums.at[slot], c_send, c_recv, {"pair": other, "rep": 1 - r}).start()
    seven = sums.at[0 : 2 * n - 1]
    remote(seven, seven, c_send, c_recv, sibling).wait_recv()
    total = sums[0]
    for s in range(1, 2 * n):
        total = total + sums[s]
    out_ref[...] = total[0:ri_here, 0 : 2 * ri_here]

    remote(seven, seven, c_send, c_recv, sibling).wait_send()
    for q in range(ri_here):
        for hop in range(n - 1):
            at_each(functools.partial(sent, q, hop))
        shared = three.at[q, pl.ds(0, reach), pl.ds(0, n - 1), core_part]
        remote(shared, shared, f_send.at[q], f_recv.at[q], sibling).wait_send()
        remote(y_buf.at[0, :, q], y_buf.at[0, :, q], y_send.at[q], y_recv.at[q], partner).wait_send()
    for s, (src, dst, device) in enumerate(halos):
        remote(src, dst, g_send.at[s], g_recv.at[s], device).wait_send()
        remote(dst, dst, h_send.at[s], h_recv.at[s], sibling).wait_send()


def one_kernel(b_int, gv_band, go_band, mask):
    n = lax.axis_size("pair")
    ri_here, nblk, rows, width = b_int.shape
    nb = gv_band.shape[0]
    half = go_band.shape[1]
    dma = pltpu.SemaphoreType.DMA
    hbm = pl.BlockSpec(memory_space=pltpu.HBM)
    per_hop, per_q = dma((ri_here, n - 1)), dma((ri_here,))
    return pl.pallas_call(
        functools.partial(fused, n),
        out_shape=jax.ShapeDtypeStruct((ri_here, 2 * ri_here), jnp.float32),
        in_specs=[hbm, hbm, hbm, hbm],
        out_specs=pl.BlockSpec(memory_space=pltpu.VMEM),
        scratch_shapes=[
            pltpu.VMEM((ri_here, nblk, n, rows, width), jnp.bfloat16),
            pltpu.VMEM((nb + 2 * R, BS, gv_band.shape[2]), jnp.bfloat16),
            pltpu.VMEM(go_band.shape, jnp.bfloat16),
            pltpu.SMEM(mask.shape[::-1], jnp.int32),
            pltpu.VMEM((2, nb, ri_here, half, WINDOW * BS), jnp.bfloat16),
            pltpu.VMEM((nb, ri_here * half, WINDOW * BS), jnp.float32),
            pltpu.VMEM((nb, ri_here * half, WINDOW * BS), jnp.bfloat16),
            pltpu.VMEM((2 * n, 8, BS), jnp.float32),
            dma((3,)), per_q, per_hop, per_hop, per_hop, per_hop, per_q, per_q,
            per_q, per_q, dma((2,)), dma((2,)), dma((2,)), dma((2,)), dma, dma,
        ],
        compiler_params=pltpu.CompilerParams(
            collective_id=0, has_side_effects=True, vmem_limit_bytes=63 * 1024 * 1024
        ),
    )(b_int, gv_band, go_band, mask.T)


def on_device(b_int, gv_band, go_band, mask):
    fits = (
        lax.axis_size("ri") == 2
        and lax.axis_size("rep") == 2
        and 2 <= lax.axis_size("pair") <= 4
        and b_int.shape[2] % 32 == 0
        and go_band.shape[1] % b_int.shape[2] == 0
        and b_int.shape[0] in (2, 4, 8)
        and gv_band.shape[0] >= R
        and gv_band.shape[0] + 2 * R <= b_int.shape[1]
    )
    return (one_kernel if fits else per_device)(b_int, gv_band, go_band, mask)


def solution(mesh):
    in_specs = (
        P(("groups", "ri"), None, "pair", None),
        P(("groups", "pair"), None, None),
        P(("groups", "pair"), "rep", None),
        P("groups", None),
    )
    out_specs = P(("groups", "ri"), None)
    return jax.shard_map(
        on_device, mesh=mesh, in_specs=in_specs, out_specs=out_specs, check_vma=False
    )
```
